32 devices in a mesh: dom: 8 (over z, core), feat: 4 (over y, x).
Axes of the slice: x: 2, y: 2, z: 4, core: 2. Of those that a mesh axis runs over, the one named last changes fastest.
Arguments:
- features_t: bfloat16 [256, 12288], P('feat', 'dom'), may hold values from -6 to 6
- weight: bfloat16 [256, 256], P(None, 'feat'), may hold values from -0.375 to 0.375
- tile_values: bfloat16 [8, 4, 16, 128, 128], P('dom'), may hold values from -0.21875 to 0.21875
- row_tiles: int32 [8, 4, 16], P('dom'), may hold values from 0 to 11
- col_tiles: int32 [8, 4, 16], P('dom'), may hold values from 0 to 11
- tile_counts: int32 [8, 4], P('dom'), may hold values from 1 to 16
- cotangent_t: bfloat16 [256, 12288], P('feat', 'dom'), may hold values from -6 to 6
Outputs:
- output_t: bfloat16 [256, 12288], P('feat', 'dom')
- weight_grad: float32 [256, 256], P(None, 'feat')
- feature_grad_t: bfloat16 [256, 12288], P('feat', 'dom')
The draws below stay inside these ranges and needn't reach their ends.
Inputs may be any that keep to these rules, and one draw needn't show every extreme that they name: Tile pairs may repeat.
All inputs are finite; a program needn't handle non-finite values.
Results may differ from the reference program's by a relative error of at most 0.011.
Values may be sent and summed in bfloat16 or wider, within the bound.
A program may use at most 64 MiB of HBM per device.

```python
import math
import jax
import jax.numpy as jnp
from jax import lax

HID = 256
TILE = 128
KMAX = 16
ROWS = 1536
STEPS = 4
NODES = 12288
N_DOM = 8


def draw_tile_counts(key, part):
    key = jax.random.fold_in(key, 7)
    load_key, slot_key = jax.random.split(key)
    load_factor = jax.random.randint(load_key, (N_DOM, 1), 2, 6)
    raw_counts = jax.random.randint(slot_key, (N_DOM, STEPS), 1, KMAX + 1)
    counts = jnp.clip(raw_counts * load_factor // 4, 1, KMAX)
    return counts.at[:, 0].set(KMAX).astype(jnp.int32)


def touch_ends(entries, stream_key, low, high):
    extent = entries.shape
    index_at = [jax.random.randint(jax.random.fold_in(stream_key, axis), (), 0, extent[axis]) for axis in range(len(extent))]
    entries = entries.at[tuple(index_at)].set(low)
    longest = extent.index(max(extent))
    index_at[longest] = (index_at[longest] + 1) % extent[longest]
    return entries.at[tuple(index_at)].set(high)


def block_levels(rng, dims, pieces, least, high):
    def one(axis_at, parts):
        heights = jax.random.uniform(jax.random.fold_in(jax.random.fold_in(rng, 6), axis_at), (parts,), jnp.float32, least / len(pieces), high / len(pieces))
        return jnp.repeat(jnp.exp(heights), dims[axis_at] // parts).reshape((-1,) + (1,) * (len(dims) - axis_at - 1))

    loudness = one(*pieces[0])
    for cut in pieces[1:]:
        loudness = loudness * one(*cut)
    return loudness


def gaussian(stream_key, extent, deviation, reach, cuts=(), kind=jnp.bfloat16):
    drawn = jax.random.normal(stream_key, extent, jnp.float32) * deviation
    if len(cuts) > 0:
        drawn = block_levels(stream_key, extent, cuts, -0.22, 0.18) * drawn
    return jnp.clip(drawn, min=-reach, max=reach).astype(kind)


def setup_inputs(seed: int = 0) -> dict:
    key_list = jax.random.split(jax.random.key(seed), 8)
    features_t = gaussian(key_list[0], (HID, NODES), 1.0, 6.0, ((0, 4), (1, 8)))
    weight = gaussian(key_list[1], (HID, HID), HID ** -0.5, 0.375, ((1, 4),))
    tile_values = gaussian(key_list[2], (N_DOM, STEPS, KMAX, TILE, TILE), (STEPS * KMAX * TILE * TILE // ROWS) ** -0.5, 0.21875, ((0, 8),))
    row_tiles = touch_ends(jax.random.randint(key_list[3], (N_DOM, STEPS, KMAX), 0, ROWS // TILE), jax.random.fold_in(key_list[3], 1), 0, (ROWS // TILE) - 1).astype(jnp.int32)
    col_tiles = touch_ends(jax.random.randint(key_list[4], (N_DOM, STEPS, KMAX), 0, ROWS // TILE), jax.random.fold_in(key_list[4], 1), 0, (ROWS // TILE) - 1).astype(jnp.int32)
    tile_counts = draw_tile_counts(jax.random.fold_in(key_list[7], 71), 0)
    cotangent_t = gaussian(key_list[6], (HID, NODES), 1.0, 6.0, ((0, 4), (1, 8)))
    return {"features_t": features_t, "weight": weight, "tile_values": tile_values, "row_tiles": row_tiles, "col_tiles": col_tiles, "tile_counts": tile_counts, "cotangent_t": cotangent_t}


def masked_table(indices, counts, table_size):
    slots = jnp.arange(indices.shape[-1], dtype=jnp.int32)
    valid = (slots < counts[..., None]).astype(jnp.float32)
    table = (indices[..., None] == jnp.arange(table_size, dtype=jnp.int32)).astype(jnp.float32)
    return table * valid[..., None]

def reference(features_t, weight, tile_values, row_tiles, col_tiles, tile_counts, cotangent_t):
    tiles_per = ROWS // TILE
    feat_blocks = features_t.reshape(HID, N_DOM, tiles_per, TILE)

    def forward_step(running, step_index):
        shifted = jnp.roll(feat_blocks, step_index, axis=1)
        col_index = col_tiles[:, step_index]
        picked = jnp.take_along_axis(shifted, col_index[None, :, :, None], axis=2)
        tile_now = tile_values[:, step_index].astype(jnp.float32)
        products = jnp.einsum('fpkc,pkrc->fpkr', picked.astype(jnp.float32), tile_now)
        scatter_table = masked_table(row_tiles[:, step_index], tile_counts[:, step_index], tiles_per)
        return (running + jnp.einsum('fpkr,pkt->fptr', products, scatter_table), None)
    start_sum = jnp.zeros((HID, N_DOM, tiles_per, TILE), jnp.float32)
    hidden_sum, _ = lax.scan(forward_step, start_sum, jnp.arange(STEPS, dtype=jnp.int32))
    hidden_t = hidden_sum.reshape(HID, NODES).astype(jnp.bfloat16)
    output_t = jnp.dot(weight.T, hidden_t, preferred_element_type=jnp.float32).astype(jnp.bfloat16)
    weight_grad = lax.dot_general(hidden_t, cotangent_t, (((1,), (1,)), ((), ())), preferred_element_type=jnp.float32)
    weight_grad = weight_grad * (1.0 / math.sqrt(NODES))
    grad_hidden = jnp.dot(weight, cotangent_t, preferred_element_type=jnp.float32).astype(jnp.bfloat16)
    grad_blocks = grad_hidden.reshape(HID, N_DOM, tiles_per, TILE)

    def backward_step(running, step_index):
        row_index = row_tiles[:, step_index]
        picked = jnp.take_along_axis(grad_blocks, row_index[None, :, :, None], axis=2)
        tile_now = tile_values[:, step_index].astype(jnp.float32)
        products = jnp.einsum('fpkr,pkrc->fpkc', picked.astype(jnp.float32), tile_now)
        scatter_table = masked_table(col_tiles[:, step_index], tile_counts[:, step_index], tiles_per)
        term = jnp.einsum('fpkc,pkt->fptc', products, scatter_table)
        return (running + jnp.roll(term, -step_index, axis=1), None)
    grad_sum, _ = lax.scan(backward_step, start_sum, jnp.arange(STEPS, dtype=jnp.int32))
    feature_grad_t = grad_sum.reshape(HID, NODES).astype(jnp.bfloat16)
    return (output_t, weight_grad, feature_grad_t)
```

```python
import functools
import math

import jax
import jax.numpy as jnp
from jax import lax
from jax.experimental import pallas as pl
from jax.experimental.pallas import tpu as pltpu
from jax.sharding import PartitionSpec as P

MESH = pl.DeviceIdType.MESH
F32 = jnp.float32
BF16 = jnp.bfloat16
VMEM_LIMIT = 40 * 1024 * 1024


def lanes(index, side):
    return pl.ds(pl.multiple_of(index * side, side), side)


def pull_kernel(row_ref, col_ref, count_ref, cot_ref, val_ref, part_ref, own_ref, acc):
    s = pl.program_id(0)
    slots, side = val_ref.shape[1], val_ref.shape[3]
    nodes = cot_ref.shape[1]
    acc[...] = jnp.zeros_like(acc)
    count = count_ref[0, s]
    for k in range(slots):
        target = jnp.where(k < count, col_ref[0, s, k], nodes // side)
        term = jnp.dot(
            cot_ref[:, lanes(row_ref[0, s, k], side)],
            val_ref[0, k],
            preferred_element_type=F32,
        )
        acc[:, lanes(target, side)] += term
    total = acc[:, :nodes]
    part_ref[0] = total.astype(BF16)

    @pl.when(s == 0)
    def _():
        own_ref[...] = total


def push_kernel(row_ref, col_ref, count_ref, got_ref, val_ref, out_ref, acc):
    s = pl.program_id(0)
    slots, side = val_ref.shape[1], val_ref.shape[3]
    nodes = out_ref.shape[1]

    @pl.when(s == 0)
    def _():
        acc[...] = jnp.zeros_like(acc)

    count = count_ref[0, s]
    for k in range(slots):
        target = jnp.where(k < count, row_ref[0, s, k], nodes // side)
        term = lax.dot_general(
            got_ref[0, :, lanes(col_ref[0, s, k], side)],
            val_ref[0, k],
            (((1,), (1,)), ((), ())),
            preferred_element_type=F32,
        )
        acc[:, lanes(target, side)] += term

    @pl.when(s == pl.num_programs(0) - 1)
    def _():
        out_ref[...] = acc[:, :nodes].astype(BF16)


def exchange_kernel(
    n_dom, n_feat, scale,
    feat_ref, weight_ref, part_ref, own_ref,
    got_ref, wgrad_ref, fgrad_ref,
    all_feat, all_grad, w_rows, sib_part, sum_part, far_part, extra_part, pieces, wgrad_t,
    w_part, f_sem, w_sem, g_sem, sib_sem, far_sem, ex_sem, y_sem, yf_sem, ye_sem, rs_sem, ag_sem,
):
    steps, width, nodes = part_ref.shape
    pairs = steps // 2 - 1
    n_red = w_part.shape[0]
    me = lax.axis_index("dom")
    mine = lax.axis_index("feat")
    odd = lax.rem(me, 2)
    sib = me + 1 - 2 * odd
    extra = jnp.where(odd == 1, 1, steps - 1)
    y_extra = jnp.where(odd == 1, steps - 1, 1)

    def dom_at(offset):
        return lax.rem(me + offset + n_dom, n_dom)

    def feat_at(offset):
        return lax.rem(mine + offset + n_feat, n_feat)

    def to_dom(src, dst, sem, index, target):
        return pltpu.make_async_remote_copy(
            src_ref=src, dst_ref=dst, send_sem=sem.at[0, index], recv_sem=sem.at[1, index],
            device_id=(target, mine), device_id_type=MESH,
        )

    def to_feat(src, dst, sem, index, target):
        return pltpu.make_async_remote_copy(
            src_ref=src, dst_ref=dst, send_sem=sem.at[0, index], recv_sem=sem.at[1, index],
            device_id=(me, target), device_id_type=MESH,
        )

    barrier = pltpu.get_barrier_semaphore()

    def greet(k, carry):
        pl.semaphore_signal(barrier, inc=1, device_id=(dom_at(k), mine), device_id_type=MESH)
        return carry

    lax.fori_loop(1, n_dom, greet, 0)
    for k in range(1, n_feat):
        pl.semaphore_signal(barrier, inc=1, device_id=(me, feat_at(k)), device_id_type=MESH)
    pl.semaphore_wait(barrier, n_dom + n_feat - 2)

    my_rows = pl.ds(pl.multiple_of(mine * width, width), width)

    sib_copies = []
    for j in range(1, pairs + 1):
        c = to_dom(part_ref.at[2 * j - 1 + 2 * odd], sib_part.at[j - 1], sib_sem, j - 1, sib)
        c.start()
        sib_copies.append(c)
    f_copies, w_copies = [], []
    for k in range(1, n_feat):
        c = to_feat(feat_ref, all_feat.at[my_rows], f_sem, k - 1, feat_at(k))
        c.start()
        f_copies.append(c)
    ex_copy = to_dom(part_ref.at[extra], extra_part, ex_sem, 0, dom_at(-extra))
    ex_copy.start()
    for k in range(1, n_feat):
        there = feat_at(k)
        rows = pl.ds(pl.multiple_of(there * width, width), width)
        c = to_feat(weight_ref.at[rows], w_rows.at[mine], w_sem, k - 1, there)
        c.start()
        w_copies.append(c)
    far_copies = []
    for j in range(1, pairs + 1):
        sib_copies[j - 1].wait_recv()
        sum_part[j - 1] = (part_ref[2 * j].astype(F32) + sib_part[j - 1].astype(F32)).astype(BF16)
        c = to_dom(sum_part.at[j - 1], far_part.at[j - 1], far_sem, j - 1, dom_at(-2 * j))
        c.start()
        far_copies.append(c)
    all_feat[my_rows] = feat_ref[...]
    w_rows[mine] = weight_ref[my_rows]

    for c in f_copies:
        c.wait_recv()
    y = lax.dot_general(
        weight_ref[...], all_feat[...], (((0,), (0,)), ((), ())), preferred_element_type=F32
    )
    got_ref[0] = y.astype(BF16)
    y_copies = []
    for j in range(1, pairs + 1):
        c = to_dom(got_ref.at[0], got_ref.at[2 * j], y_sem, j - 1, dom_at(2 * j))
        c.start()
        y_copies.append(c)
    ye_copy = to_dom(got_ref.at[0], got_ref.at[y_extra], ye_sem, 0, dom_at(y_extra))
    ye_copy.start()

    total = own_ref[...]
    for j in range(1, pairs + 1):
        far_copies[j - 1].wait_recv()
        total += far_part[j - 1].astype(F32)
    ex_copy.wait_recv()
    total += extra_part[...].astype(F32)
    all_grad[my_rows] = total.astype(BF16)
    g_copies = []
    for k in range(1, n_feat):
        c = to_feat(all_grad.at[my_rows], all_grad.at[my_rows], g_sem, k - 1, feat_at(k))
        c.start()
        g_copies.append(c)
    w_term = lax.dot_general(
        all_grad[my_rows], all_feat[...], (((1,), (1,)), ((), ())), preferred_element_type=F32
    )
    for i in range(n_red):
        w_part[i] = w_term[8 * i:8 * i + 8]

    def when(cond, run):
        if cond is None:
            run()
        else:
            pl.when(cond)(run)

    def reducer(index):
        return None if n_red == n_dom else index < n_red

    def rs_copy(k):
        there = dom_at(k)
        piece = there if n_red == n_dom else lax.rem(there, n_red)
        return to_dom(w_part.at[piece], pieces.at[me], rs_sem, k - 1, there)

    def ag_copy(k):
        piece = me if n_red == n_dom else lax.rem(me, n_red)
        return to_dom(wgrad_t.at[piece], wgrad_t.at[piece], ag_sem, k - 1, dom_at(k))

    def each(make):
        def step(k, carry):
            make(k)
            return carry

        lax.fori_loop(1, n_dom, step, 0)

    each(lambda k: when(reducer(dom_at(k)), lambda: rs_copy(k).start()))

    yf_copies = []
    for j in range(1, pairs + 1):
        y_copies[j - 1].wait_recv()
        c = to_dom(got_ref.at[2 * j], got_ref.at[2 * j + 1 - 2 * odd], yf_sem, j - 1, sib)
        c.start()
        yf_copies.append(c)

    def reduce_piece():
        piece = me if n_red == n_dom else lax.rem(me, n_red)
        pieces[me] = w_part[piece]
        each(lambda k: rs_copy(k).wait_recv())
        wgrad_t[piece] = jnp.sum(pieces[...], axis=0) * scale
        each(lambda k: ag_copy(k).start())

    when(reducer(me), reduce_piece)

    for c in w_copies + g_copies:
        c.wait_recv()
    w_mine = jnp.concatenate([w_rows[k] for k in range(n_feat)], axis=1)
    fgrad_ref[...] = jnp.dot(w_mine, all_grad[...], preferred_element_type=F32).astype(BF16)

    each(lambda k: when(reducer(dom_at(-k)), lambda: ag_copy(k).wait_recv()))
    wgrad_ref[...] = wgrad_t[...].reshape(width, -1).T

    for c in yf_copies + [ye_copy]:
        c.wait_recv()
    for c in sib_copies + f_copies + w_copies + far_copies + [ex_copy] + y_copies + [ye_copy]:
        c.wait_send()
    for c in g_copies + yf_copies:
        c.wait_send()
    each(lambda k: when(reducer(dom_at(k)), lambda: rs_copy(k).wait_send()))
    when(reducer(me), lambda: each(lambda k: ag_copy(k).wait_send()))


def body(n_dom, n_feat, features_t, weight, tile_values, row_tiles, col_tiles, tile_counts, cotangent_t):
    width, nodes = features_t.shape
    hid = weight.shape[0]
    _, steps, slots, side, _ = tile_values.shape
    values = tile_values[0]
    smem = pl.BlockSpec(memory_space=pltpu.SMEM)
    vmem = pl.BlockSpec(memory_space=pltpu.VMEM)
    tile_spec = pl.BlockSpec((1, slots, side, side), lambda s: (s, 0, 0, 0))
    step_spec = pl.BlockSpec((1, width, nodes), lambda s: (s, 0, 0))
    full_spec = pl.BlockSpec((width, nodes), lambda s: (0, 0))
    acc = pltpu.VMEM((width, nodes + side), F32)

    part, own = pl.pallas_call(
        pull_kernel,
        grid=(steps,),
        out_shape=(
            jax.ShapeDtypeStruct((steps, width, nodes), BF16),
            jax.ShapeDtypeStruct((width, nodes), F32),
        ),
        in_specs=[smem, smem, smem, full_spec, tile_spec],
        out_specs=(step_spec, full_spec),
        scratch_shapes=[acc],
        compiler_params=pltpu.CompilerParams(vmem_limit_bytes=VMEM_LIMIT),
        name="pull",
    )(row_tiles, col_tiles, tile_counts, cotangent_t, values)

    pairs = steps // 2 - 1
    n_red = min(width // 8, n_dom)

    def sems(count):
        return pltpu.SemaphoreType.DMA((2, count))

    got, weight_grad, feature_grad_t = pl.pallas_call(
        functools.partial(exchange_kernel, n_dom, n_feat, 1.0 / math.sqrt(nodes * n_dom)),
        out_shape=(
            jax.ShapeDtypeStruct((steps, width, nodes), BF16),
            jax.ShapeDtypeStruct((hid, width), F32),
            jax.ShapeDtypeStruct((width, nodes), BF16),
        ),
        in_specs=[vmem] * 4,
        out_specs=(vmem,) * 3,
        scratch_shapes=[
            pltpu.VMEM((hid, nodes), BF16),
            pltpu.VMEM((hid, nodes), BF16),
            pltpu.VMEM((n_feat, width, width), BF16),
            pltpu.VMEM((pairs, width, nodes), BF16),
            pltpu.VMEM((pairs, width, nodes), BF16),
            pltpu.VMEM((pairs, width, nodes), BF16),
            pltpu.VMEM((width, nodes), BF16),
            pltpu.VMEM((n_dom, 8, hid), F32),
            pltpu.VMEM((n_red, 8, hid), F32),
            pltpu.VMEM((n_red, 8, hid), F32),
            sems(n_feat - 1), sems(n_feat - 1), sems(n_feat - 1),
            sems(pairs), sems(pairs), sems(1),
            sems(pairs), sems(pairs), sems(1),
            sems(n_dom - 1), sems(n_dom - 1),
        ],
        compiler_params=pltpu.CompilerParams(
            vmem_limit_bytes=VMEM_LIMIT, collective_id=0, has_side_effects=True
        ),
        name="exchange",
    )(features_t, weight, part, own)

    output_t = pl.pallas_call(
        push_kernel,
        grid=(steps,),
        out_shape=jax.ShapeDtypeStruct((width, nodes), BF16),
        in_specs=[smem, smem, smem, step_spec, tile_spec],
        out_specs=full_spec,
        scratch_shapes=[acc],
        compiler_params=pltpu.CompilerParams(vmem_limit_bytes=VMEM_LIMIT),
        name="push",
    )(row_tiles, col_tiles, tile_counts, got, values)
    return output_t, weight_grad, feature_grad_t


def solution(mesh):
    in_specs = (
        P("feat", "dom"),
        P(None, "feat"),
        P("dom", None, None, None, None),
        P("dom", None, None),
        P("dom", None, None),
        P("dom", None),
        P("feat", "dom"),
    )
    out_specs = (P("feat", "dom"), P(None, "feat"), P("feat", "dom"))
    local = functools.partial(body, mesh.shape["dom"], mesh.shape["feat"])
    return jax.shard_map(local, mesh=mesh, in_specs=in_specs, out_specs=out_specs, check_vma=False)
```

```python
import functools
import math

import jax
import jax.numpy as jnp
from jax import lax
from jax.experimental import pallas as pl
from jax.experimental.pallas import tpu as pltpu
from jax.sharding import PartitionSpec as P

MESH = pl.DeviceIdType.MESH
F32 = jnp.float32
BF16 = jnp.bfloat16
VMEM_LIMIT = 40 * 1024 * 1024


def lanes(index, side):
    return pl.ds(pl.multiple_of(index * side, side), side)


def pull_kernel(
    row_hbm, col_hbm, count_hbm, cot_hbm, val_hbm, part_ref, own_ref,
    row_ref, col_ref, count_ref, cot_ref, val_ref, acc, sem, val_sem,
):
    steps, slots, side = val_ref.shape[0], val_ref.shape[1], val_ref.shape[3]
    nodes = cot_ref.shape[1]
    small = [
        pltpu.make_async_copy(src, dst, sem.at[i])
        for i, (src, dst) in enumerate(
            [(row_hbm, row_ref), (col_hbm, col_ref), (count_hbm, count_ref), (cot_hbm, cot_ref)]
        )
    ]
    for c in small:
        c.start()

    def val_copy(s):
        return pltpu.make_async_copy(val_hbm.at[s], val_ref.at[s], val_sem.at[s])

    for s in range(steps):
        val_copy(s).start()
    for c in small:
        c.wait()

    def one(s, carry):
        acc[...] = jnp.zeros_like(acc)
        count = count_ref[0, s]
        val_copy(s).wait()
        for k in range(slots):
            target = jnp.where(k < count, col_ref[0, s, k], nodes // side)
            term = jnp.dot(
                cot_ref[:, lanes(row_ref[0, s, k], side)],
                val_ref[s, k],
                preferred_element_type=F32,
            )
            acc[:, lanes(target, side)] += term
        total = acc[:, :nodes]
        part_ref[s] = total.astype(BF16)

        @pl.when(s == 0)
        def _():
            own_ref[...] = total

        return carry

    lax.fori_loop(0, steps, one, 0)


def push_kernel(row_ref, col_ref, count_ref, got_ref, val_ref, out_ref, acc):
    steps, slots, side = val_ref.shape[0], val_ref.shape[1], val_ref.shape[3]
    nodes = out_ref.shape[1]
    acc[...] = jnp.zeros_like(acc)

    def one(s, carry):
        count = count_ref[0, s]
        for k in range(slots):
            target = jnp.where(k < count, row_ref[0, s, k], nodes // side)
            term = lax.dot_general(
                got_ref[s, :, lanes(col_ref[0, s, k], side)],
                val_ref[s, k],
                (((1,), (1,)), ((), ())),
                preferred_element_type=F32,
            )
            acc[:, lanes(target, side)] += term
        return carry

    lax.fori_loop(0, steps, one, 0)
    out_ref[...] = acc[:, :nodes].astype(BF16)


def exchange_kernel(
    n_dom, n_feat, scale,
    feat_ref, weight_ref, part_ref, own_ref,
    got_ref, wgrad_ref, fgrad_ref,
    all_feat, all_grad, w_cols, sib_part, sum_part, far_part, extra_part, pieces, wgrad_t,
    w_part, w_out, f_sem, w_sem, g_sem, sib_sem, far_sem, ex_sem, y_sem, yf_sem, ye_sem, rs_sem, ag_sem,
):
    steps, width, nodes = part_ref.shape
    pairs = steps // 2 - 1
    n_red = w_part.shape[0]
    me = lax.axis_index("dom")
    mine = lax.axis_index("feat")
    odd = lax.rem(me, 2)
    sib = me + 1 - 2 * odd
    extra = jnp.where(odd == 1, 1, steps - 1)
    y_extra = jnp.where(odd == 1, steps - 1, 1)

    def dom_at(offset):
        return lax.rem(me + offset + n_dom, n_dom)

    def feat_at(offset):
        return lax.rem(mine + offset + n_feat, n_feat)

    def to_dom(src, dst, sem, index, target):
        return pltpu.make_async_remote_copy(
            src_ref=src, dst_ref=dst, send_sem=sem.at[0, index], recv_sem=sem.at[1, index],
            device_id=(target, mine), device_id_type=MESH,
        )

    def to_feat(src, dst, sem, index, target):
        return pltpu.make_async_remote_copy(
            src_ref=src, dst_ref=dst, send_sem=sem.at[0, index], recv_sem=sem.at[1, index],
            device_id=(me, target), device_id_type=MESH,
        )

    barrier = pltpu.get_barrier_semaphore()

    def greet(k, carry):
        pl.semaphore_signal(barrier, inc=1, device_id=(dom_at(k), mine), device_id_type=MESH)
        return carry

    lax.fori_loop(1, n_dom, greet, 0)
    for k in range(1, n_feat):
        pl.semaphore_signal(barrier, inc=1, device_id=(me, feat_at(k)), device_id_type=MESH)
    pl.semaphore_wait(barrier, n_dom + n_feat - 2)

    half = width // 2
    group = n_feat // 2
    high = feat_at(group)
    base = lax.div(mine, group) * group

    def low(offset):
        return base + lax.rem(mine - base + offset + group, group)

    def gather(buf, sem):
        def copy(block, part, index, target):
            rows = buf.at[pl.ds(pl.multiple_of(block * width + part * half, half), half)]
            return to_feat(rows, rows, sem, index, target)

        near = [
            [copy(mine, h, 2 * (k - 1) + h, low(k)) for h in range(2)] for k in range(1, group)
        ]
        across = [copy(mine, h, 2 * (group - 1) + h, high) for h in range(2)]
        pass_high = [copy(low(-k), 0, 2 * group + k - 1, high) for k in range(1, group)]
        pass_near = [copy(high, 1, 3 * group + k - 2, low(k)) for k in range(1, group)]
        every = [c for two in near for c in two] + across + pass_high + pass_near

        def begin():
            for k in range(group - 1):
                near[k][0].start()
            across[1].start()
            for k in range(group - 1):
                near[k][1].start()
            across[0].start()

        def forward():
            for k in range(group - 1):
                near[k][0].wait_recv()
                pass_high[k].start()
            across[1].wait_recv()
            for c in pass_near:
                c.start()

        def arrive():
            for k in range(group - 1):
                near[k][1].wait_recv()
            across[0].wait_recv()
            for c in pass_high + pass_near:
                c.wait_recv()

        def sent():
            for c in every:
                c.wait_send()

        return begin, forward, arrive, sent

    my_rows = pl.ds(pl.multiple_of(mine * width, width), width)

    sib_copies = []
    for j in range(1, pairs + 1):
        c = to_dom(part_ref.at[2 * j - 1 + 2 * odd], sib_part.at[j - 1], sib_sem, j - 1, sib)
        c.start()
        sib_copies.append(c)
    all_feat[my_rows] = feat_ref[...]
    f_begin, f_forward, f_arrive, f_sent = gather(all_feat, f_sem)
    g_begin, g_forward, g_arrive, g_sent = gather(all_grad, g_sem)
    f_begin()
    far_copies = []
    for j in range(1, pairs + 1):
        sib_copies[j - 1].wait_recv()
        sum_part[j - 1] = (part_ref[2 * j].astype(F32) + sib_part[j - 1].astype(F32)).astype(BF16)
        c = to_dom(sum_part.at[j - 1], far_part.at[j - 1], far_sem, j - 1, dom_at(-2 * j))
        c.start()
        far_copies.append(c)
    ex_copy = to_dom(part_ref.at[extra], extra_part, ex_sem, 0, dom_at(-extra))
    ex_copy.start()
    weight = weight_ref[...].T
    for k in range(n_feat):
        w_out[k] = weight[k * width:(k + 1) * width]
    w_copies = []
    for k in range(1, n_feat):
        c = to_feat(w_out.at[feat_at(k)], w_cols.at[mine], w_sem, k - 1, feat_at(k))
        c.start()
        w_copies.append(c)
    w_cols[mine] = w_out[mine]
    f_forward()

    total = own_ref[...]
    for j in range(1, pairs + 1):
        far_copies[j - 1].wait_recv()
        total += far_part[j - 1].astype(F32)
    ex_copy.wait_recv()
    total += extra_part[...].astype(F32)
    all_grad[my_rows] = total.astype(BF16)
    f_arrive()
    g_begin()

    y = jnp.dot(weight_ref[...], all_feat[...], preferred_element_type=F32)
    got_ref[0] = y.astype(BF16)
    y_copies = []
    for j in range(1, pairs + 1):
        c = to_dom(got_ref.at[0], got_ref.at[2 * j], y_sem, j - 1, dom_at(2 * j))
        c.start()
        y_copies.append(c)

    w_term = lax.dot_general(
        all_grad[my_rows], all_feat[...], (((1,), (1,)), ((), ())), preferred_element_type=F32
    )
    for i in range(n_red):
        w_part[i] = w_term[8 * i:8 * i + 8]

    def when(cond, run):
        if cond is None:
            run()
        else:
            pl.when(cond)(run)

    def reducer(index):
        return None if n_red == n_dom else index < n_red

    my_piece = me if n_red == n_dom else lax.rem(me, n_red)

    def rs_copy(k):
        there = dom_at(k)
        piece = there if n_red == n_dom else lax.rem(there, n_red)
        return to_dom(w_part.at[piece], pieces.at[me], rs_sem, k - 1, there)

    def ag_copy(k):
        return to_dom(wgrad_t.at[my_piece], wgrad_t.at[my_piece], ag_sem, k - 1, dom_at(k))

    def each(make):
        def step(k, carry):
            make(k)
            return carry

        lax.fori_loop(1, n_dom, step, 0)

    each(lambda k: when(reducer(dom_at(k)), lambda: rs_copy(k).start()))
    ye_copy = to_dom(got_ref.at[0], got_ref.at[y_extra], ye_sem, 0, dom_at(y_extra))
    ye_copy.start()
    g_forward()

    def reduce_piece():
        pieces[me] = w_part[my_piece]
        each(lambda k: rs_copy(k).wait_recv())
        wgrad_t[my_piece] = jnp.sum(pieces[...], axis=0) * scale
        each(lambda k: ag_copy(k).start())

    when(reducer(me), reduce_piece)

    yf_copies = []
    for j in range(1, pairs + 1):
        y_copies[j - 1].wait_recv()
        c = to_dom(got_ref.at[2 * j], got_ref.at[2 * j + 1 - 2 * odd], yf_sem, j - 1, sib)
        c.start()
        yf_copies.append(c)

    for c in w_copies:
        c.wait_recv()
    w_mine = jnp.concatenate([w_cols[k] for k in range(n_feat)], axis=1)
    g_arrive()
    fgrad_ref[...] = jnp.dot(w_mine, all_grad[...], preferred_element_type=F32).astype(BF16)

    each(lambda k: when(reducer(dom_at(-k)), lambda: ag_copy(k).wait_recv()))
    wgrad_ref[...] = wgrad_t[...].reshape(wgrad_ref.shape)

    for c in yf_copies + [ye_copy]:
        c.wait_recv()
    for c in sib_copies + w_copies + far_copies + [ex_copy] + y_copies + [ye_copy] + yf_copies:
        c.wait_send()
    f_sent()
    g_sent()
    each(lambda k: when(reducer(dom_at(k)), lambda: rs_copy(k).wait_send()))
    when(reducer(me), lambda: each(lambda k: ag_copy(k).wait_send()))


def body(n_dom, n_feat, features_t, weight, tile_values, row_tiles, col_tiles, tile_counts, cotangent_t):
    width, nodes = features_t.shape
    hid = weight.shape[0]
    _, steps, slots, side, _ = tile_values.shape
    values = tile_values[0]
    smem = pl.BlockSpec(memory_space=pltpu.SMEM)
    vmem = pl.BlockSpec(memory_space=pltpu.VMEM)
    hbm = pl.BlockSpec(memory_space=pltpu.HBM)
    acc = pltpu.VMEM((width, nodes + side), F32)

    part, own = pl.pallas_call(
        pull_kernel,
        out_shape=(
            jax.ShapeDtypeStruct((steps, width, nodes), BF16),
            jax.ShapeDtypeStruct((width, nodes), F32),
        ),
        in_specs=[hbm] * 5,
        out_specs=(vmem, vmem),
        scratch_shapes=[
            pltpu.SMEM(row_tiles.shape, jnp.int32),
            pltpu.SMEM(col_tiles.shape, jnp.int32),
            pltpu.SMEM(tile_counts.shape, jnp.int32),
            pltpu.VMEM((width, nodes), BF16),
            pltpu.VMEM(values.shape, BF16),
            acc,
            pltpu.SemaphoreType.DMA((4,)),
            pltpu.SemaphoreType.DMA((steps,)),
        ],
        compiler_params=pltpu.CompilerParams(vmem_limit_bytes=VMEM_LIMIT),
        name="pull",
    )(row_tiles, col_tiles, tile_counts, cotangent_t, values)

    pairs = steps // 2 - 1
    n_red = min(width // 8, n_dom)

    def sems(count):
        return pltpu.SemaphoreType.DMA((2, count))

    got, weight_grad, feature_grad_t = pl.pallas_call(
        functools.partial(exchange_kernel, n_dom, n_feat, 1.0 / math.sqrt(nodes * n_dom)),
        out_shape=(
            jax.ShapeDtypeStruct((steps, width, nodes), BF16),
            jax.ShapeDtypeStruct((width, hid), F32),
            jax.ShapeDtypeStruct((width, nodes), BF16),
        ),
        in_specs=[vmem] * 4,
        out_specs=(vmem,) * 3,
        scratch_shapes=[
            pltpu.VMEM((hid, nodes), BF16),
            pltpu.VMEM((hid, nodes), BF16),
            pltpu.VMEM((n_feat, width, width), BF16),
            pltpu.VMEM((pairs, width, nodes), BF16),
            pltpu.VMEM((pairs, width, nodes), BF16),
            pltpu.VMEM((pairs, width, nodes), BF16),
            pltpu.VMEM((width, nodes), BF16),
            pltpu.VMEM((n_dom, 8, hid), F32),
            pltpu.VMEM((n_red, 8, hid), F32),
            pltpu.VMEM((n_red, 8, hid), F32),
            pltpu.VMEM((n_feat, width, width), BF16),
            sems(2 * n_feat - 2), sems(n_feat - 1), sems(2 * n_feat - 2),
            sems(pairs), sems(pairs), sems(1),
            sems(pairs), sems(pairs), sems(1),
            sems(n_dom - 1), sems(n_dom - 1),
        ],
        compiler_params=pltpu.CompilerParams(
            vmem_limit_bytes=VMEM_LIMIT, collective_id=0, has_side_effects=True
        ),
        name="exchange",
    )(features_t, weight.T, part, own)

    output_t = pl.pallas_call(
        push_kernel,
        out_shape=jax.ShapeDtypeStruct((width, nodes), BF16),
        in_specs=[smem, smem, smem, vmem, vmem],
        out_specs=vmem,
        scratch_shapes=[acc],
        compiler_params=pltpu.CompilerParams(vmem_limit_bytes=VMEM_LIMIT),
        name="push",
    )(row_tiles, col_tiles, tile_counts, got, values)
    return output_t, weight_grad.T, feature_grad_t


def solution(mesh):
    in_specs = (
        P("feat", "dom"),
        P(None, "feat"),
        P("dom", None, None, None, None),
        P("dom", None, None),
        P("dom", None, None),
        P("dom", None),
        P("feat", "dom"),
    )
    out_specs = (P("feat", "dom"), P(None, "feat"), P("feat", "dom"))
    local = functools.partial(body, mesh.shape["dom"], mesh.shape["feat"])
    return jax.shard_map(local, mesh=mesh, in_specs=in_specs, out_specs=out_specs, check_vma=False)
```

```python
import functools
import math

import jax
import jax.numpy as jnp
from jax import lax
from jax.experimental import pallas as pl
from jax.experimental.pallas import tpu as pltpu
from jax.sharding import PartitionSpec as P

MESH = pl.DeviceIdType.MESH
F32 = jnp.float32
BF16 = jnp.bfloat16
VMEM_LIMIT = 40 * 1024 * 1024
PULL_LIMIT = 62 * 1024 * 1024
CUTS = 3
PIECE = 16


def lanes(index, side):
    return pl.ds(pl.multiple_of(index * side, side), side)


def pull_kernel(
    row_hbm, col_hbm, count_hbm, cot_hbm, val_hbm, part_ref, own_ref,
    row_ref, col_ref, count_ref, cot_ref, val_ref, acc, sem, val_sem,
):
    steps, slots, side = val_ref.shape[0], val_ref.shape[1], val_ref.shape[3]
    nodes = cot_ref.shape[1]
    small = [
        pltpu.make_async_copy(src, dst, sem.at[i])
        for i, (src, dst) in enumerate(
            [(row_hbm, row_ref), (col_hbm, col_ref), (count_hbm, count_ref), (cot_hbm, cot_ref)]
        )
    ]
    for c in small:
        c.start()

    def val_copy(s):
        return pltpu.make_async_copy(val_hbm.at[s], val_ref.at[s], val_sem.at[s])

    for s in range(steps):
        val_copy(s).start()
    for c in small:
        c.wait()

    def one(s, carry):
        acc[...] = jnp.zeros_like(acc)
        count = count_ref[0, s]
        val_copy(s).wait()
        for k in range(slots):
            target = jnp.where(k < count, col_ref[0, s, k], nodes // side)
            term = jnp.dot(
                cot_ref[:, lanes(row_ref[0, s, k], side)],
                val_ref[s, k],
                preferred_element_type=F32,
            )
            acc[:, lanes(target, side)] += term
        total = acc[:, :nodes]
        part_ref[s] = total.astype(BF16)

        @pl.when(s == 0)
        def _():
            own_ref[...] = total

        return carry

    lax.fori_loop(0, steps, one, 0)


def push_kernel(row_ref, col_ref, count_ref, got_ref, val_ref, out_ref, acc):
    steps, slots, side = val_ref.shape[0], val_ref.shape[1], val_ref.shape[3]
    nodes = out_ref.shape[1]
    acc[...] = jnp.zeros_like(acc)

    def one(s, carry):
        count = count_ref[0, s]
        for k in range(slots):
            target = jnp.where(k < count, row_ref[0, s, k], nodes // side)
            term = lax.dot_general(
                got_ref[s, :, lanes(col_ref[0, s, k], side)],
                val_ref[s, k],
                (((1,), (1,)), ((), ())),
                preferred_element_type=F32,
            )
            acc[:, lanes(target, side)] += term
        return carry

    lax.fori_loop(0, steps, one, 0)
    out_ref[...] = acc[:, :nodes].astype(BF16)


def exchange_kernel(
    n_dom, n_feat, scale,
    feat_ref, weight_ref, part_ref, own_ref,
    got_ref, wgrad_ref, fgrad_ref,
    all_feat, all_grad, w_cols, sib_part, sum_part, far_part, extra_part, pieces, wgrad_t,
    w_part, w_out, f_sem, w_sem, g_sem, sib_sem, far_sem, ex_sem, y_sem, yf_sem, ye_sem, rs_sem, ag_sem,
):
    steps, width, nodes = part_ref.shape
    pairs = steps // 2 - 1
    n_red = w_part.shape[0]
    me = lax.axis_index("dom")
    mine = lax.axis_index("feat")
    odd = lax.rem(me, 2)
    sib = me + 1 - 2 * odd
    extra = jnp.where(odd == 1, 1, steps - 1)
    y_extra = jnp.where(odd == 1, steps - 1, 1)

    def dom_at(offset):
        return lax.rem(me + offset + n_dom, n_dom)

    def feat_at(offset):
        return lax.rem(mine + offset + n_feat, n_feat)

    def to_dom(src, dst, sem, index, target):
        return pltpu.make_async_remote_copy(
            src_ref=src, dst_ref=dst, send_sem=sem.at[0, index], recv_sem=sem.at[1, index],
            device_id=(target, mine), device_id_type=MESH,
        )

    def to_feat(src, dst, sem, index, target):
        return pltpu.make_async_remote_copy(
            src_ref=src, dst_ref=dst, send_sem=sem.at[0, index], recv_sem=sem.at[1, index],
            device_id=(me, target), device_id_type=MESH,
        )

    barrier = pltpu.get_barrier_semaphore()

    def greet(k, carry):
        pl.semaphore_signal(barrier, inc=1, device_id=(dom_at(k), mine), device_id_type=MESH)
        return carry

    lax.fori_loop(1, n_dom, greet, 0)
    for k in range(1, n_feat):
        pl.semaphore_signal(barrier, inc=1, device_id=(me, feat_at(k)), device_id_type=MESH)
    pl.semaphore_wait(barrier, n_dom + n_feat - 2)

    half = width // 2
    group = n_feat // 2
    high = feat_at(group)
    base = lax.div(mine, group) * group

    def low(offset):
        return base + lax.rem(mine - base + offset + group, group)

    def gather(buf, sem):
        def copy(block, part, index, target):
            rows = buf.at[pl.ds(pl.multiple_of(block * width + part * half, half), half)]
            return to_feat(rows, rows, sem, index, target)

        near = [
            [copy(mine, h, 2 * (k - 1) + h, low(k)) for h in range(2)] for k in range(1, group)
        ]
        across = [copy(mine, h, 2 * (group - 1) + h, high) for h in range(2)]
        pass_high = [copy(low(-k), 0, 2 * group + k - 1, high) for k in range(1, group)]
        pass_near = [copy(high, 1, 3 * group + k - 2, low(k)) for k in range(1, group)]
        every = [c for two in near for c in two] + across + pass_high + pass_near

        def begin():
            for k in range(group - 1):
                near[k][0].start()
            across[1].start()
            for k in range(group - 1):
                near[k][1].start()
            across[0].start()

        def forward():
            for k in range(group - 1):
                near[k][0].wait_recv()
                pass_high[k].start()
            across[1].wait_recv()
            for c in pass_near:
                c.start()

        def arrive():
            for k in range(group - 1):
                near[k][1].wait_recv()
            across[0].wait_recv()
            for c in pass_high + pass_near:
                c.wait_recv()

        def sent():
            for c in every:
                c.wait_send()

        return begin, forward, arrive, sent

    my_rows = pl.ds(pl.multiple_of(mine * width, width), width)

    sib_copies = []
    for j in range(1, pairs + 1):
        c = to_dom(part_ref.at[2 * j - 1 + 2 * odd], sib_part.at[j - 1], sib_sem, j - 1, sib)
        c.start()
        sib_copies.append(c)
    ex_copy = to_dom(part_ref.at[extra], extra_part, ex_sem, 0, dom_at(-extra))
    ex_copy.start()
    all_feat[my_rows] = feat_ref[...]
    f_begin, f_forward, f_arrive, f_sent = gather(all_feat, f_sem)
    g_begin, g_forward, g_arrive, g_sent = gather(all_grad, g_sem)
    f_begin()
    far_copies = []
    for j in range(1, pairs + 1):
        sib_copies[j - 1].wait_recv()
        sum_part[j - 1] = (part_ref[2 * j].astype(F32) + sib_part[j - 1].astype(F32)).astype(BF16)
        c = to_dom(sum_part.at[j - 1], far_part.at[j - 1], far_sem, j - 1, dom_at(-2 * j))
        c.start()
        far_copies.append(c)
    weight = weight_ref[...].T
    for k in range(n_feat):
        w_out[k] = weight[k * width:(k + 1) * width]
    w_copies = []
    for k in range(1, n_feat):
        c = to_feat(w_out.at[feat_at(k)], w_cols.at[mine], w_sem, k - 1, feat_at(k))
        c.start()
        w_copies.append(c)
    w_cols[mine] = w_out[mine]
    f_forward()

    cut = nodes // CUTS
    y_copies = [[] for _ in range(pairs)]
    ye_copies = []
    f_arrive()
    for i in range(CUTS):
        cols = pl.ds(i * cut, cut)
        y = jnp.dot(weight_ref[...], all_feat[:, cols], preferred_element_type=F32)
        got_ref[0, :, cols] = y.astype(BF16)
        here = got_ref.at[0, :, cols]
        c = to_dom(here, got_ref.at[y_extra, :, cols], ye_sem, i, dom_at(y_extra))
        c.start()
        ye_copies.append(c)
        for j in range(1, pairs + 1):
            c = to_dom(here, got_ref.at[2 * j, :, cols], y_sem, (j - 1) * CUTS + i, dom_at(2 * j))
            c.start()
            y_copies[j - 1].append(c)

    total = own_ref[...]
    ex_copy.wait_recv()
    total += extra_part[...].astype(F32)
    for j in range(1, pairs + 1):
        far_copies[j - 1].wait_recv()
        total += far_part[j - 1].astype(F32)
    all_grad[my_rows] = total.astype(BF16)
    g_begin()

    w_term = lax.dot_general(
        all_grad[my_rows], all_feat[...], (((1,), (1,)), ((), ())), preferred_element_type=F32
    )
    for i in range(n_red):
        w_part[i] = w_term[PIECE * i:PIECE * i + PIECE].astype(BF16)

    def when(cond, run):
        if cond is None:
            run()
        else:
            pl.when(cond)(run)

    stride = n_dom // n_red

    def reducer(index):
        return None if stride == 1 else lax.rem(index, stride) == 0

    my_piece = lax.div(me, stride)

    def rs_copy(k):
        there = dom_at(k)
        return to_dom(w_part.at[lax.div(there, stride)], pieces.at[me], rs_sem, k - 1, there)

    def ag_copy(k):
        return to_dom(wgrad_t.at[my_piece], wgrad_t.at[my_piece], ag_sem, k - 1, dom_at(k))

    def each(make):
        def step(k, carry):
            make(k)
            return carry

        lax.fori_loop(1, n_dom, step, 0)

    each(lambda k: when(reducer(dom_at(k)), lambda: rs_copy(k).start()))
    g_forward()

    def reduce_piece():
        pieces[me] = w_part[my_piece]
        each(lambda k: rs_copy(k).wait_recv())
        wgrad_t[my_piece] = (jnp.sum(pieces[...].astype(F32), axis=0) * scale).astype(BF16)
        each(lambda k: ag_copy(k).start())

    when(reducer(me), reduce_piece)

    yf_copies = []
    for i in range(CUTS):
        cols = pl.ds(i * cut, cut)
        for j in range(1, pairs + 1):
            y_copies[j - 1][i].wait_recv()
            c = to_dom(
                got_ref.at[2 * j, :, cols], got_ref.at[2 * j + 1 - 2 * odd, :, cols],
                yf_sem, (j - 1) * CUTS + i, sib,
            )
            c.start()
            yf_copies.append(c)

    for c in w_copies:
        c.wait_recv()
    w_mine = jnp.concatenate([w_cols[k] for k in range(n_feat)], axis=1)
    g_arrive()
    fgrad_ref[...] = jnp.dot(w_mine, all_grad[...], preferred_element_type=F32).astype(BF16)

    each(lambda k: when(reducer(dom_at(-k)), lambda: ag_copy(k).wait_recv()))
    wgrad_ref[...] = wgrad_t[...].astype(F32).reshape(wgrad_ref.shape)

    for c in yf_copies + ye_copies:
        c.wait_recv()
    for c in sib_copies + w_copies + far_copies + [ex_copy] + sum(y_copies, []) + ye_copies + yf_copies:
        c.wait_send()
    f_sent()
    g_sent()
    each(lambda k: when(reducer(dom_at(k)), lambda: rs_copy(k).wait_send()))
    when(reducer(me), lambda: each(lambda k: ag_copy(k).wait_send()))


def body(n_dom, n_feat, features_t, weight, tile_values, row_tiles, col_tiles, tile_counts, cotangent_t):
    width, nodes = features_t.shape
    hid = weight.shape[0]
    _, steps, slots, side, _ = tile_values.shape
    values = tile_values[0]
    smem = pl.BlockSpec(memory_space=pltpu.SMEM)
    vmem = pl.BlockSpec(memory_space=pltpu.VMEM)
    hbm = pl.BlockSpec(memory_space=pltpu.HBM)
    acc = pltpu.VMEM((width, nodes + side), F32)

    part, own = pl.pallas_call(
        pull_kernel,
        out_shape=(
            jax.ShapeDtypeStruct((steps, width, nodes), BF16),
            jax.ShapeDtypeStruct((width, nodes), F32),
        ),
        in_specs=[hbm] * 5,
        out_specs=(vmem, vmem),
        scratch_shapes=[
            pltpu.SMEM(row_tiles.shape, jnp.int32),
            pltpu.SMEM(col_tiles.shape, jnp.int32),
            pltpu.SMEM(tile_counts.shape, jnp.int32),
            pltpu.VMEM((width, nodes), BF16),
            pltpu.VMEM(values.shape, BF16),
            acc,
            pltpu.SemaphoreType.DMA((4,)),
            pltpu.SemaphoreType.DMA((steps,)),
        ],
        compiler_params=pltpu.CompilerParams(vmem_limit_bytes=PULL_LIMIT),
        name="pull",
    )(row_tiles, col_tiles, tile_counts, cotangent_t, values)

    pairs = steps // 2 - 1
    n_red = min(width // PIECE, n_dom)

    def sems(count):
        return pltpu.SemaphoreType.DMA((2, count))

    got, weight_grad, feature_grad_t = pl.pallas_call(
        functools.partial(exchange_kernel, n_dom, n_feat, 1.0 / math.sqrt(nodes * n_dom)),
        out_shape=(
            jax.ShapeDtypeStruct((steps, width, nodes), BF16),
            jax.ShapeDtypeStruct((width, hid), F32),
            jax.ShapeDtypeStruct((width, nodes), BF16),
        ),
        in_specs=[vmem] * 4,
        out_specs=(vmem,) * 3,
        scratch_shapes=[
            pltpu.VMEM((hid, nodes), BF16),
            pltpu.VMEM((hid, nodes), BF16),
            pltpu.VMEM((n_feat, width, width), BF16),
            pltpu.VMEM((pairs, width, nodes), BF16),
            pltpu.VMEM((pairs, width, nodes), BF16),
            pltpu.VMEM((pairs, width, nodes), BF16),
            pltpu.VMEM((width, nodes), BF16),
            pltpu.VMEM((n_dom, PIECE, hid), BF16),
            pltpu.VMEM((n_red, PIECE, hid), BF16),
            pltpu.VMEM((n_red, PIECE, hid), BF16),
            pltpu.VMEM((n_feat, width, width), BF16),
            sems(2 * n_feat - 2), sems(n_feat - 1), sems(2 * n_feat - 2),
            sems(pairs), sems(pairs), sems(1),
            sems(pairs * CUTS), sems(pairs * CUTS), sems(CUTS),
            sems(n_dom - 1), sems(n_dom - 1),
        ],
        compiler_params=pltpu.CompilerParams(
            vmem_limit_bytes=VMEM_LIMIT, collective_id=0, has_side_effects=True
        ),
        name="exchange",
    )(features_t, weight.T, part, own)

    output_t = pl.pallas_call(
        push_kernel,
        out_shape=jax.ShapeDtypeStruct((width, nodes), BF16),
        in_specs=[smem, smem, smem, vmem, vmem],
        out_specs=vmem,
        scratch_shapes=[acc],
        compiler_params=pltpu.CompilerParams(vmem_limit_bytes=VMEM_LIMIT),
        name="push",
    )(row_tiles, col_tiles, tile_counts, got, values)
    return output_t, weight_grad.T, feature_grad_t


def solution(mesh):
    in_specs = (
        P("feat", "dom"),
        P(None, "feat"),
        P("dom", None, None, None, None),
        P("dom", None, None),
        P("dom", None, None),
        P("dom", None),
        P("feat", "dom"),
    )
    out_specs = (P("feat", "dom"), P(None, "feat"), P("feat", "dom"))
    local = functools.partial(body, mesh.shape["dom"], mesh.shape["feat"])
    return jax.shard_map(local, mesh=mesh, in_specs=in_specs, out_specs=out_specs, check_vma=False)
```

```python
import functools
import math

import jax
import jax.numpy as jnp
from jax import lax
from jax.experimental import pallas as pl
from jax.experimental.pallas import tpu as pltpu
from jax.sharding import PartitionSpec as P

MESH = pl.DeviceIdType.MESH
F32 = jnp.float32
BF16 = jnp.bfloat16
VMEM_LIMIT = 40 * 1024 * 1024
PULL_LIMIT = 62 * 1024 * 1024
CUTS = 1
PIECE = 16


def lanes(index, side):
    return pl.ds(pl.multiple_of(index * side, side), side)


def pull_kernel(
    row_hbm, col_hbm, count_hbm, cot_hbm, val_hbm, part_ref,
    row_ref, col_ref, count_ref, cot_ref, val_ref, acc, sem, val_sem,
):
    steps, slots, side = val_ref.shape[0], val_ref.shape[1], val_ref.shape[3]
    nodes = cot_ref.shape[1]
    small = [
        pltpu.make_async_copy(src, dst, sem.at[i])
        for i, (src, dst) in enumerate(
            [(row_hbm, row_ref), (col_hbm, col_ref), (count_hbm, count_ref), (cot_hbm, cot_ref)]
        )
    ]
    for c in small:
        c.start()

    def val_copy(s):
        return pltpu.make_async_copy(val_hbm.at[s], val_ref.at[s], val_sem.at[s])

    for s in range(steps):
        val_copy(s).start()
    for c in small:
        c.wait()

    def one(s, carry):
        acc[...] = jnp.zeros_like(acc)
        count = count_ref[0, s]
        val_copy(s).wait()
        for k in range(slots):
            target = jnp.where(k < count, col_ref[0, s, k], nodes // side)
            term = jnp.dot(
                cot_ref[:, lanes(row_ref[0, s, k], side)],
                val_ref[s, k],
                preferred_element_type=F32,
            )
            acc[:, lanes(target, side)] += term
        total = acc[:, :nodes]
        part_ref[s] = total.astype(BF16)
        return carry

    lax.fori_loop(0, steps, one, 0)


def push_kernel(row_ref, col_ref, count_ref, got_ref, val_ref, out_ref, acc):
    steps, slots, side = val_ref.shape[0], val_ref.shape[1], val_ref.shape[3]
    nodes = out_ref.shape[1]
    acc[...] = jnp.zeros_like(acc)

    def one(s, carry):
        count = count_ref[0, s]
        for k in range(slots):
            target = jnp.where(k < count, row_ref[0, s, k], nodes // side)
            term = lax.dot_general(
                got_ref[s, :, lanes(col_ref[0, s, k], side)],
                val_ref[s, k],
                (((1,), (1,)), ((), ())),
                preferred_element_type=F32,
            )
            acc[:, lanes(target, side)] += term
        return carry

    lax.fori_loop(0, steps, one, 0)
    out_ref[...] = acc[:, :nodes].astype(BF16)


def exchange_kernel(
    n_dom, n_feat, scale,
    feat_ref, weight_ref, part_ref,
    got_ref, wgrad_ref, fgrad_ref,
    all_feat, all_grad, w_cols, sib_part, sum_part, far_part, extra_part, pieces, wgrad_t,
    w_part, w_out, f_sem, w_sem, g_sem, sib_sem, far_sem, ex_sem, y_sem, yf_sem, ye_sem, rs_sem, ag_sem,
):
    steps, width, nodes = part_ref.shape
    pairs = steps // 2 - 1
    n_red = w_part.shape[0]
    me = lax.axis_index("dom")
    mine = lax.axis_index("feat")
    odd = lax.rem(me, 2)
    sib = me + 1 - 2 * odd
    extra = jnp.where(odd == 1, 1, steps - 1)

    def dom_at(offset):
        return lax.rem(me + offset + n_dom, n_dom)

    def feat_at(offset):
        return lax.rem(mine + offset + n_feat, n_feat)

    def to_dom(src, dst, sem, index, target):
        return pltpu.make_async_remote_copy(
            src_ref=src, dst_ref=dst, send_sem=sem.at[0, index], recv_sem=sem.at[1, index],
            device_id=(target, mine), device_id_type=MESH,
        )

    def to_feat(src, dst, sem, index, target):
        return pltpu.make_async_remote_copy(
            src_ref=src, dst_ref=dst, send_sem=sem.at[0, index], recv_sem=sem.at[1, index],
            device_id=(me, target), device_id_type=MESH,
        )

    barrier = pltpu.get_barrier_semaphore()

    def greet(k, carry):
        pl.semaphore_signal(barrier, inc=1, device_id=(dom_at(k), mine), device_id_type=MESH)
        return carry

    lax.fori_loop(1, n_dom, greet, 0)
    for k in range(1, n_feat):
        pl.semaphore_signal(barrier, inc=1, device_id=(me, feat_at(k)), device_id_type=MESH)
    pl.semaphore_wait(barrier, n_dom + n_feat - 2)

    half = width // 2
    group = n_feat // 2
    high = feat_at(group)
    base = lax.div(mine, group) * group

    def low(offset):
        return base + lax.rem(mine - base + offset + group, group)

    def gather(buf, sem):
        def copy(block, part, index, target):
            rows = buf.at[pl.ds(pl.multiple_of(block * width + part * half, half), half)]
            return to_feat(rows, rows, sem, index, target)

        near = [
            [copy(mine, h, 2 * (k - 1) + h, low(k)) for h in range(2)] for k in range(1, group)
        ]
        across = [copy(mine, h, 2 * (group - 1) + h, high) for h in range(2)]
        pass_high = [copy(low(-k), 0, 2 * group + k - 1, high) for k in range(1, group)]
        pass_near = [copy(high, 1, 3 * group + k - 2, low(k)) for k in range(1, group)]
        every = [c for two in near for c in two] + across + pass_high + pass_near

        def begin():
            for k in range(group - 1):
                near[k][0].start()
            across[1].start()
            for k in range(group - 1):
                near[k][1].start()
            across[0].start()

        def forward():
            for k in range(group - 1):
                near[k][0].wait_recv()
                pass_high[k].start()
            across[1].wait_recv()
            for c in pass_near:
                c.start()

        def arrive():
            for k in range(group - 1):
                near[k][1].wait_recv()
            across[0].wait_recv()
            for c in pass_high + pass_near:
                c.wait_recv()

        def sent():
            for c in every:
                c.wait_send()

        return begin, forward, arrive, sent

    my_rows = pl.ds(pl.multiple_of(mine * width, width), width)

    sib_copies = []
    for j in range(1, pairs + 1):
        c = to_dom(part_ref.at[2 * j - 1 + 2 * odd], sib_part.at[j - 1], sib_sem, j - 1, sib)
        c.start()
        sib_copies.append(c)
    all_feat[my_rows] = feat_ref[...]
    f_begin, f_forward, f_arrive, f_sent = gather(all_feat, f_sem)
    g_begin, g_forward, g_arrive, g_sent = gather(all_grad, g_sem)
    f_begin()
    far_copies = []
    for j in range(1, pairs + 1):
        sib_copies[j - 1].wait_recv()
        sum_part[j - 1] = (part_ref[2 * j].astype(F32) + sib_part[j - 1].astype(F32)).astype(BF16)
        c = to_dom(sum_part.at[j - 1], far_part.at[j - 1], far_sem, j - 1, dom_at(-2 * j))
        c.start()
        far_copies.append(c)
    ex_copy = to_dom(part_ref.at[extra], extra_part, ex_sem, 0, dom_at(-extra))
    ex_copy.start()
    weight = weight_ref[...].T
    for k in range(n_feat):
        w_out[k] = weight[k * width:(k + 1) * width]
    w_copies = []
    for k in range(1, n_feat):
        c = to_feat(w_out.at[feat_at(k)], w_cols.at[mine], w_sem, k - 1, feat_at(k))
        c.start()
        w_copies.append(c)
    w_cols[mine] = w_out[mine]
    f_forward()

    cut = nodes // CUTS
    y_copies = [[] for _ in range(pairs)]
    total = part_ref[0].astype(F32)
    ex_copy.wait_recv()
    total += extra_part[...].astype(F32)
    for j in range(1, pairs + 1):
        far_copies[j - 1].wait_recv()
        total += far_part[j - 1].astype(F32)
    all_grad[my_rows] = total.astype(BF16)

    f_arrive()
    g_begin()
    for i in range(CUTS):
        cols = pl.ds(i * cut, cut)
        y = jnp.dot(weight_ref[...], all_feat[:, cols], preferred_element_type=F32)
        got_ref[0, :, cols] = y.astype(BF16)
        here = got_ref.at[0, :, cols]
        for j in range(1, pairs + 1):
            c = to_dom(here, got_ref.at[2 * j, :, cols], y_sem, (j - 1) * CUTS + i, dom_at(2 * j))
            c.start()
            y_copies[j - 1].append(c)

    w_term = lax.dot_general(
        all_grad[my_rows], all_feat[...], (((1,), (1,)), ((), ())), preferred_element_type=F32
    )
    for i in range(n_red):
        w_part[i] = w_term[PIECE * i:PIECE * i + PIECE].astype(BF16)

    def when(cond, run):
        if cond is None:
            run()
        else:
            pl.when(cond)(run)

    stride = n_dom // n_red

    def reducer(index):
        return None if stride == 1 else lax.rem(index, stride) == 0

    my_piece = lax.div(me, stride)

    def rs_copy(k):
        there = dom_at(k)
        return to_dom(w_part.at[lax.div(there, stride)], pieces.at[me], rs_sem, k - 1, there)

    def ag_copy(k):
        return to_dom(wgrad_t.at[my_piece], wgrad_t.at[my_piece], ag_sem, k - 1, dom_at(k))

    def each(make):
        def step(k, carry):
            make(k)
            return carry

        lax.fori_loop(1, n_dom, step, 0)

    each(lambda k: when(reducer(dom_at(k)), lambda: rs_copy(k).start()))
    g_forward()

    def reduce_piece():
        pieces[me] = w_part[my_piece]
        each(lambda k: rs_copy(k).wait_recv())
        wgrad_t[my_piece] = (jnp.sum(pieces[...].astype(F32), axis=0) * scale).astype(BF16)
        each(lambda k: ag_copy(k).start())

    when(reducer(me), reduce_piece)

    yf_copies = []
    for i in range(CUTS):
        cols = pl.ds(i * cut, cut)
        for j in range(1, pairs + 1):
            y_copies[j - 1][i].wait_recv()
            c = to_dom(
                got_ref.at[2 * j, :, cols], got_ref.at[2 * j + 1 - 2 * odd, :, cols],
                yf_sem, (j - 1) * CUTS + i, sib,
            )
            c.start()
            yf_copies.append(c)

    ye_from = jnp.where(odd == 1, steps - 2, 0)
    ye_copies = [to_dom(got_ref.at[ye_from], got_ref.at[ye_from + 1], ye_sem, 0, dom_at(1))]
    ye_copies[0].start()

    for c in w_copies:
        c.wait_recv()
    w_mine = jnp.concatenate([w_cols[k] for k in range(n_feat)], axis=1)
    g_arrive()
    fgrad_ref[...] = jnp.dot(w_mine, all_grad[...], preferred_element_type=F32).astype(BF16)

    each(lambda k: when(reducer(dom_at(-k)), lambda: ag_copy(k).wait_recv()))
    wgrad_ref[...] = wgrad_t[...].astype(F32).reshape(wgrad_ref.shape)

    for c in yf_copies + ye_copies:
        c.wait_recv()
    for c in sib_copies + w_copies + far_copies + [ex_copy] + sum(y_copies, []) + ye_copies + yf_copies:
        c.wait_send()
    f_sent()
    g_sent()
    each(lambda k: when(reducer(dom_at(k)), lambda: rs_copy(k).wait_send()))
    when(reducer(me), lambda: each(lambda k: ag_copy(k).wait_send()))


def body(n_dom, n_feat, features_t, weight, tile_values, row_tiles, col_tiles, tile_counts, cotangent_t):
    width, nodes = features_t.shape
    hid = weight.shape[0]
    _, steps, slots, side, _ = tile_values.shape
    values = tile_values[0]
    smem = pl.BlockSpec(memory_space=pltpu.SMEM)
    vmem = pl.BlockSpec(memory_space=pltpu.VMEM)
    hbm = pl.BlockSpec(memory_space=pltpu.HBM)
    acc = pltpu.VMEM((width, nodes + side), F32)

    part = pl.pallas_call(
        pull_kernel,
        out_shape=jax.ShapeDtypeStruct((steps, width, nodes), BF16),
        in_specs=[hbm] * 5,
        out_specs=vmem,
        scratch_shapes=[
            pltpu.SMEM(row_tiles.shape, jnp.int32),
            pltpu.SMEM(col_tiles.shape, jnp.int32),
            pltpu.SMEM(tile_counts.shape, jnp.int32),
            pltpu.VMEM((width, nodes), BF16),
            pltpu.VMEM(values.shape, BF16),
            acc,
            pltpu.SemaphoreType.DMA((4,)),
            pltpu.SemaphoreType.DMA((steps,)),
        ],
        compiler_params=pltpu.CompilerParams(vmem_limit_bytes=PULL_LIMIT),
        name="pull",
    )(row_tiles, col_tiles, tile_counts, cotangent_t, values)

    pairs = steps // 2 - 1
    n_red = min(width // PIECE, n_dom)

    def sems(count):
        return pltpu.SemaphoreType.DMA((2, count))

    got, weight_grad, feature_grad_t = pl.pallas_call(
        functools.partial(exchange_kernel, n_dom, n_feat, 1.0 / math.sqrt(nodes * n_dom)),
        out_shape=(
            jax.ShapeDtypeStruct((steps, width, nodes), BF16),
            jax.ShapeDtypeStruct((width, hid), F32),
            jax.ShapeDtypeStruct((width, nodes), BF16),
        ),
        in_specs=[vmem] * 3,
        out_specs=(vmem,) * 3,
        scratch_shapes=[
            pltpu.VMEM((hid, nodes), BF16),
            pltpu.VMEM((hid, nodes), BF16),
            pltpu.VMEM((n_feat, width, width), BF16),
            pltpu.VMEM((pairs, width, nodes), BF16),
            pltpu.VMEM((pairs, width, nodes), BF16),
            pltpu.VMEM((pairs, width, nodes), BF16),
            pltpu.VMEM((width, nodes), BF16),
            pltpu.VMEM((n_dom, PIECE, hid), BF16),
            pltpu.VMEM((n_red, PIECE, hid), BF16),
            pltpu.VMEM((n_red, PIECE, hid), BF16),
            pltpu.VMEM((n_feat, width, width), BF16),
            sems(2 * n_feat - 2), sems(n_feat - 1), sems(2 * n_feat - 2),
            sems(pairs), sems(pairs), sems(1),
            sems(pairs * CUTS), sems(pairs * CUTS), sems(CUTS),
            sems(n_dom - 1), sems(n_dom - 1),
        ],
        compiler_params=pltpu.CompilerParams(
            vmem_limit_bytes=VMEM_LIMIT, collective_id=0, has_side_effects=True
        ),
        name="exchange",
    )(features_t, weight.T, part)

    output_t = pl.pallas_call(
        push_kernel,
        out_shape=jax.ShapeDtypeStruct((width, nodes), BF16),
        in_specs=[smem, smem, smem, vmem, vmem],
        out_specs=vmem,
        scratch_shapes=[acc],
        compiler_params=pltpu.CompilerParams(vmem_limit_bytes=VMEM_LIMIT),
        name="push",
    )(row_tiles, col_tiles, tile_counts, got, values)
    return output_t, weight_grad.T, feature_grad_t


def solution(mesh):
    in_specs = (
        P("feat", "dom"),
        P(None, "feat"),
        P("dom", None, None, None, None),
        P("dom", None, None),
        P("dom", None, None),
        P("dom", None),
        P("feat", "dom"),
    )
    out_specs = (P("feat", "dom"), P(None, "feat"), P("feat", "dom"))
    local = functools.partial(body, mesh.shape["dom"], mesh.shape["feat"])
    return jax.shard_map(local, mesh=mesh, in_specs=in_specs, out_specs=out_specs, check_vma=False)
```

```python
import functools
import math

import jax
import jax.numpy as jnp
from jax import lax
from jax.experimental import pallas as pl
from jax.experimental.pallas import tpu as pltpu
from jax.sharding import PartitionSpec as P

MESH = pl.DeviceIdType.MESH
F32 = jnp.float32
BF16 = jnp.bfloat16
VMEM_LIMIT = 40 * 1024 * 1024
PULL_LIMIT = 58 * 1024 * 1024
CUTS = 1
PIECE = 16


def lanes(index, side):
    return pl.ds(pl.multiple_of(index * side, side), side)


def pull_kernel(
    row_hbm, col_hbm, count_hbm, cot_hbm, val_hbm, part_ref,
    row_ref, col_ref, count_ref, cot_ref, val_ref, acc, sem, val_sem,
):
    steps, slots, side = val_ref.shape[0], val_ref.shape[1], val_ref.shape[3]
    nodes = cot_ref.shape[1]
    small = [
        pltpu.make_async_copy(src, dst, sem.at[i])
        for i, (src, dst) in enumerate(
            [(row_hbm, row_ref), (col_hbm, col_ref), (count_hbm, count_ref), (cot_hbm, cot_ref)]
        )
    ]
    for c in small:
        c.start()

    def val_copy(s):
        return pltpu.make_async_copy(val_hbm.at[s], val_ref.at[s], val_sem.at[s])

    for s in range(steps):
        val_copy(s).start()
    for c in small:
        c.wait()

    def one(s, carry):
        acc[...] = jnp.zeros_like(acc)
        count = count_ref[0, s]
        val_copy(s).wait()
        for k in range(slots):
            target = jnp.where(k < count, col_ref[0, s, k], nodes // side)
            term = jnp.dot(
                cot_ref[:, lanes(row_ref[0, s, k], side)],
                val_ref[s, k],
                preferred_element_type=F32,
            )
            acc[:, lanes(target, side)] += term
        total = acc[:, :nodes]
        part_ref[s] = total.astype(BF16)
        return carry

    lax.fori_loop(0, steps, one, 0)


def push_kernel(row_ref, col_ref, count_ref, got_ref, val_ref, out_ref, acc):
    steps, slots, side = val_ref.shape[0], val_ref.shape[1], val_ref.shape[3]
    nodes = out_ref.shape[1]
    acc[...] = jnp.zeros_like(acc)

    def one(s, carry):
        count = count_ref[0, s]
        for k in range(slots):
            target = jnp.where(k < count, row_ref[0, s, k], nodes // side)
            term = lax.dot_general(
                got_ref[s, :, lanes(col_ref[0, s, k], side)],
                val_ref[s, k],
                (((1,), (1,)), ((), ())),
                preferred_element_type=F32,
            )
            acc[:, lanes(target, side)] += term
        return carry

    lax.fori_loop(0, steps, one, 0)
    out_ref[...] = acc[:, :nodes].astype(BF16)


def exchange_kernel(
    n_dom, n_feat, scale,
    feat_ref, weight_ref, part_ref,
    got_ref, wgrad_ref, fgrad_ref,
    all_feat, all_grad, w_cols, sib_part, sum_part, far_part, extra_part, pieces, wgrad_t,
    w_part, w_out, f_sem, w_sem, g_sem, sib_sem, far_sem, ex_sem, y_sem, yf_sem, ye_sem, rs_sem, ag_sem,
):
    steps, width, nodes = part_ref.shape
    pairs = steps // 2 - 1
    n_red = w_part.shape[0]
    me = lax.axis_index("dom")
    mine = lax.axis_index("feat")
    odd = lax.rem(me, 2)
    sib = me + 1 - 2 * odd
    extra = jnp.where(odd == 1, 1, steps - 1)

    def dom_at(offset):
        return lax.rem(me + offset + n_dom, n_dom)

    def feat_at(offset):
        return lax.rem(mine + offset + n_feat, n_feat)

    def to_dom(src, dst, sem, index, target):
        return pltpu.make_async_remote_copy(
            src_ref=src, dst_ref=dst, send_sem=sem.at[0, index], recv_sem=sem.at[1, index],
            device_id=(target, mine), device_id_type=MESH,
        )

    def to_feat(src, dst, sem, index, target):
        return pltpu.make_async_remote_copy(
            src_ref=src, dst_ref=dst, send_sem=sem.at[0, index], recv_sem=sem.at[1, index],
            device_id=(me, target), device_id_type=MESH,
        )

    barrier = pltpu.get_barrier_semaphore()

    def greet(k, carry):
        pl.semaphore_signal(barrier, inc=1, device_id=(dom_at(k), mine), device_id_type=MESH)
        return carry

    lax.fori_loop(1, n_dom, greet, 0)
    for k in range(1, n_feat):
        pl.semaphore_signal(barrier, inc=1, device_id=(me, feat_at(k)), device_id_type=MESH)
    pl.semaphore_wait(barrier, n_dom + n_feat - 2)

    half = width // 2
    group = n_feat // 2
    high = feat_at(group)
    base = lax.div(mine, group) * group

    def low(offset):
        return base + lax.rem(mine - base + offset + group, group)

    def gather(buf, sem):
        def copy(block, part, index, target):
            rows = buf.at[pl.ds(pl.multiple_of(block * width + part * half, half), half)]
            return to_feat(rows, rows, sem, index, target)

        near = [
            [copy(mine, h, 2 * (k - 1) + h, low(k)) for h in range(2)] for k in range(1, group)
        ]
        across = [copy(mine, h, 2 * (group - 1) + h, high) for h in range(2)]
        pass_high = [copy(low(-k), 0, 2 * group + k - 1, high) for k in range(1, group)]
        pass_near = [copy(high, 1, 3 * group + k - 2, low(k)) for k in range(1, group)]
        every = [c for two in near for c in two] + across + pass_high + pass_near

        def begin():
            for k in range(group - 1):
                near[k][0].start()
            across[1].start()
            for k in range(group - 1):
                near[k][1].start()
            across[0].start()

        def forward():
            for k in range(group - 1):
                near[k][0].wait_recv()
                pass_high[k].start()
            across[1].wait_recv()
            for c in pass_near:
                c.start()

        def arrive():
            for k in range(group - 1):
                near[k][1].wait_recv()
            across[0].wait_recv()
            for c in pass_high + pass_near:
                c.wait_recv()

        def sent():
            for c in every:
                c.wait_send()

        return begin, forward, arrive, sent

    my_rows = pl.ds(pl.multiple_of(mine * width, width), width)

    sib_copies = []
    for j in range(1, pairs + 1):
        c = to_dom(part_ref.at[2 * j - 1 + 2 * odd], sib_part.at[j - 1], sib_sem, j - 1, sib)
        c.start()
        sib_copies.append(c)
    all_feat[my_rows] = feat_ref[...]
    f_begin, f_forward, f_arrive, f_sent = gather(all_feat, f_sem)
    g_begin, g_forward, g_arrive, g_sent = gather(all_grad, g_sem)
    f_begin()
    far_copies = []
    for j in range(1, pairs + 1):
        sib_copies[j - 1].wait_recv()
        sum_part[j - 1] = (part_ref[2 * j].astype(F32) + sib_part[j - 1].astype(F32)).astype(BF16)
        c = to_dom(sum_part.at[j - 1], far_part.at[j - 1], far_sem, j - 1, dom_at(-2 * j))
        c.start()
        far_copies.append(c)
    ex_copy = to_dom(part_ref.at[extra], extra_part, ex_sem, 0, dom_at(-extra))
    ex_copy.start()
    weight = weight_ref[...].T
    for k in range(n_feat):
        w_out[k] = weight[k * width:(k + 1) * width]
    w_copies = []
    for k in range(1, n_feat):
        c = to_feat(w_out.at[feat_at(k)], w_cols.at[mine], w_sem, k - 1, feat_at(k))
        c.start()
        w_copies.append(c)
    w_cols[mine] = w_out[mine]
    f_forward()

    cut = nodes // CUTS
    y_copies = [[] for _ in range(pairs)]
    total = part_ref[0].astype(F32)
    ex_copy.wait_recv()
    total += extra_part[...].astype(F32)
    for j in range(1, pairs + 1):
        far_copies[j - 1].wait_recv()
        total += far_part[j - 1].astype(F32)
    all_grad[my_rows] = total.astype(BF16)

    f_arrive()
    g_begin()
    for i in range(CUTS):
        cols = pl.ds(i * cut, cut)
        y = jnp.dot(weight_ref[...], all_feat[:, cols], preferred_element_type=F32)
        got_ref[0, :, cols] = y.astype(BF16)
        here = got_ref.at[0, :, cols]
        for j in range(1, pairs + 1):
            c = to_dom(here, got_ref.at[2 * j, :, cols], y_sem, (j - 1) * CUTS + i, dom_at(2 * j))
            c.start()
            y_copies[j - 1].append(c)

    w_term = lax.dot_general(
        all_grad[my_rows], all_feat[...], (((1,), (1,)), ((), ())), preferred_element_type=F32
    )
    for i in range(n_red):
        w_part[i] = w_term[PIECE * i:PIECE * i + PIECE].astype(BF16)

    def when(cond, run):
        if cond is None:
            run()
        else:
            pl.when(cond)(run)

    stride = n_dom // n_red

    def reducer(index):
        return None if stride == 1 else lax.rem(index, stride) == 0

    my_piece = lax.div(me, stride)

    def rs_copy(k):
        there = dom_at(k)
        return to_dom(w_part.at[lax.div(there, stride)], pieces.at[me], rs_sem, k - 1, there)

    def ag_copy(k):
        return to_dom(wgrad_t.at[my_piece], wgrad_t.at[my_piece], ag_sem, k - 1, dom_at(k))

    def each(make):
        def step(k, carry):
            make(k)
            return carry

        lax.fori_loop(1, n_dom, step, 0)

    each(lambda k: when(reducer(dom_at(k)), lambda: rs_copy(k).start()))
    g_forward()

    def reduce_piece():
        pieces[me] = w_part[my_piece]
        each(lambda k: rs_copy(k).wait_recv())
        wgrad_t[my_piece] = (jnp.sum(pieces[...].astype(F32), axis=0) * scale).astype(BF16)
        each(lambda k: ag_copy(k).start())

    when(reducer(me), reduce_piece)

    yf_copies = []
    for i in range(CUTS):
        cols = pl.ds(i * cut, cut)
        for j in range(1, pairs + 1):
            y_copies[j - 1][i].wait_recv()
            c = to_dom(
                got_ref.at[2 * j, :, cols], got_ref.at[2 * j + 1 - 2 * odd, :, cols],
                yf_sem, (j - 1) * CUTS + i, sib,
            )
            c.start()
            yf_copies.append(c)

    ye_from = jnp.where(odd == 1, steps - 2, 0)
    ye_copies = [to_dom(got_ref.at[ye_from], got_ref.at[ye_from + 1], ye_sem, 0, dom_at(1))]
    ye_copies[0].start()

    for c in w_copies:
        c.wait_recv()
    w_mine = jnp.concatenate([w_cols[k] for k in range(n_feat)], axis=1)
    g_arrive()
    fgrad_ref[...] = jnp.dot(w_mine, all_grad[...], preferred_element_type=F32).astype(BF16)

    each(lambda k: when(reducer(dom_at(-k)), lambda: ag_copy(k).wait_recv()))
    wgrad_ref[...] = wgrad_t[...].astype(F32).reshape(wgrad_ref.shape)

    for c in yf_copies + ye_copies:
        c.wait_recv()
    for c in sib_copies + w_copies + far_copies + [ex_copy] + sum(y_copies, []) + ye_copies + yf_copies:
        c.wait_send()
    f_sent()
    g_sent()
    each(lambda k: when(reducer(dom_at(k)), lambda: rs_copy(k).wait_send()))
    when(reducer(me), lambda: each(lambda k: ag_copy(k).wait_send()))


def body(n_dom, n_feat, features_t, weight, tile_values, row_tiles, col_tiles, tile_counts, cotangent_t):
    width, nodes = features_t.shape
    hid = weight.shape[0]
    _, steps, slots, side, _ = tile_values.shape
    values = tile_values[0]
    smem = pl.BlockSpec(memory_space=pltpu.SMEM)
    vmem = pl.BlockSpec(memory_space=pltpu.VMEM)
    hbm = pl.BlockSpec(memory_space=pltpu.HBM)
    acc = pltpu.VMEM((width, nodes + side), F32)

    part = pl.pallas_call(
        pull_kernel,
        out_shape=jax.ShapeDtypeStruct((steps, width, nodes), BF16),
        in_specs=[hbm] * 5,
        out_specs=vmem,
        scratch_shapes=[
            pltpu.SMEM(row_tiles.shape, jnp.int32),
            pltpu.SMEM(col_tiles.shape, jnp.int32),
            pltpu.SMEM(tile_counts.shape, jnp.int32),
            pltpu.VMEM((width, nodes), BF16),
            pltpu.VMEM(values.shape, BF16),
            acc,
            pltpu.SemaphoreType.DMA((4,)),
            pltpu.SemaphoreType.DMA((steps,)),
        ],
        compiler_params=pltpu.CompilerParams(vmem_limit_bytes=PULL_LIMIT),
        name="pull",
    )(row_tiles, col_tiles, tile_counts, cotangent_t, values)

    pairs = steps // 2 - 1
    n_red = min(width // PIECE, n_dom)

    def sems(count):
        return pltpu.SemaphoreType.DMA((2, count))

    got, weight_grad, feature_grad_t = pl.pallas_call(
        functools.partial(exchange_kernel, n_dom, n_feat, 1.0 / math.sqrt(nodes * n_dom)),
        out_shape=(
            jax.ShapeDtypeStruct((steps, width, nodes), BF16),
            jax.ShapeDtypeStruct((width, hid), F32),
            jax.ShapeDtypeStruct((width, nodes), BF16),
        ),
        in_specs=[vmem] * 3,
        out_specs=(vmem,) * 3,
        scratch_shapes=[
            pltpu.VMEM((hid, nodes), BF16),
            pltpu.VMEM((hid, nodes), BF16),
            pltpu.VMEM((n_feat, width, width), BF16),
            pltpu.VMEM((pairs, width, nodes), BF16),
            pltpu.VMEM((pairs, width, nodes), BF16),
            pltpu.VMEM((pairs, width, nodes), BF16),
            pltpu.VMEM((width, nodes), BF16),
            pltpu.VMEM((n_dom, PIECE, hid), BF16),
            pltpu.VMEM((n_red, PIECE, hid), BF16),
            pltpu.VMEM((n_red, PIECE, hid), BF16),
            pltpu.VMEM((n_feat, width, width), BF16),
            sems(2 * n_feat - 2), sems(n_feat - 1), sems(2 * n_feat - 2),
            sems(pairs), sems(pairs), sems(1),
            sems(pairs * CUTS), sems(pairs * CUTS), sems(CUTS),
            sems(n_dom - 1), sems(n_dom - 1),
        ],
        compiler_params=pltpu.CompilerParams(
            vmem_limit_bytes=VMEM_LIMIT, collective_id=0, has_side_effects=True
        ),
        name="exchange",
    )(features_t, weight.T, part)

    output_t = pl.pallas_call(
        push_kernel,
        out_shape=jax.ShapeDtypeStruct((width, nodes), BF16),
        in_specs=[smem, smem, smem, vmem, vmem],
        out_specs=vmem,
        scratch_shapes=[acc],
        compiler_params=pltpu.CompilerParams(vmem_limit_bytes=VMEM_LIMIT),
        name="push",
    )(row_tiles, col_tiles, tile_counts, got, values)
    return output_t, weight_grad.T, feature_grad_t


def solution(mesh):
    in_specs = (
        P("feat", "dom"),
        P(None, "feat"),
        P("dom", None, None, None, None),
        P("dom", None, None),
        P("dom", None, None),
        P("dom", None),
        P("feat", "dom"),
    )
    out_specs = (P("feat", "dom"), P(None, "feat"), P("feat", "dom"))
    local = functools.partial(body, mesh.shape["dom"], mesh.shape["feat"])
    return jax.shard_map(local, mesh=mesh, in_specs=in_specs, out_specs=out_specs, check_vma=False)
```
